256 devices in a mesh: gx: 16 (over z, core), gy: 4 (over x), gz: 4 (over y).
Axes of the slice: x: 4, y: 4, z: 8, core: 2. Of those that a mesh axis runs over, the one named last changes fastest.
Arguments:
- sim_density: float32 [128, 8, 128, 512], P('gx', None, 'gy', 'gz'), may hold values from 0.002 to 3, as said below
- brick_home: int32 [128, 4, 4], P('gx', 'gy', 'gz'), may hold values from 0 to 127, as said below
- jitter: int32 [1024, 128], P('gx', 'gy'), may hold values from 0 to 15
Outputs:
- image: float32 [2, 256, 32], P(None, 'gx', ('gy', 'gz'))
The draws below stay inside these ranges and needn't reach their ends.
Inputs may be any that keep to these rules, and one draw needn't show every extreme that they name: `brick_home`: within each group of equal second and third indices the entries are a permutation; entry h places the brick on the gx device h // 8 at slot h % 8. That device lies at most 2 positions away along gx, counted cyclically; no device sends more than 2 bricks to one device (itself included), some device of every group sends exactly 2, and all devices of a group send equally many bricks to the device a given number of positions further. `sim_density`: a positive density.
All inputs are finite; a program needn't handle non-finite values.
Results may differ from the reference program's by a relative error of at most 0.0001.
Values sent between devices are 32-bit elements; how exact they have to be, the bound alone decides.
No kernel may reach another device: no remote copies, remote signals or barrier semaphores. Data moves between devices by JAX's collectives and lax.ppermute only.
A program may use at most 64 MiB of HBM per device.

```python
import jax
import jax.numpy as jnp

NBR = 8
BX = 8
CY = 32
CZ = 128
STRIDE = 16
MT = 8
PIXEL = 4
REACH = 2
OFFS = 5
CAP = 2
BRICKS = 128
NX = 1024
NY = 128
NZ = 512
NCOL = 32
N_GX = 16
N_GY = 4
N_GZ = 4


def draw_sim_density(key, part):
    key = jax.random.fold_in(key, 11)
    key_rough, key_scale = jax.random.split(key)
    roughness = jnp.exp(jax.random.uniform(key_rough, (BRICKS, BX, NY, NZ), jnp.float32, jnp.log(0.05), 0.0))
    scales = jnp.exp(jax.random.uniform(key_scale, (BRICKS, 1, NY // MT, 1, 16, 1), jnp.float32, jnp.log(0.1), 0.0))
    height = (jnp.arange(NY, dtype=jnp.float32) + 0.5) / NY
    profile = 0.4 + 0.3 * (1.0 + jnp.tanh((height - 0.5) * 6.0))
    depth_ramp = 1.0 + 2.0 * jnp.arange(NZ, dtype=jnp.float32) / NZ
    shaped = (roughness.reshape(BRICKS, BX, NY // MT, MT, 16, NZ // 16) * scales).reshape(BRICKS, BX, NY, NZ)
    return shaped * profile[None, None, :, None] * depth_ramp


def permute_slots(item_key):
    return jax.random.permutation(item_key, NBR).astype(jnp.int32)


def group_homes(group_key):
    shift_values = []
    for step_value in range(-REACH, REACH + 1):
        if step_value % N_GX not in shift_values:
            shift_values.append(step_value % N_GX)
    shift_table = jnp.array(shift_values, jnp.int32)
    key_lead, key_rest, key_slots, key_sim = jax.random.split(group_key, 4)
    leading = jax.random.randint(key_lead, (), 0, OFFS).astype(jnp.int32)
    others = jnp.arange((OFFS - 1) * CAP, dtype=jnp.int32) // CAP
    others = others + (others >= leading).astype(jnp.int32)
    remaining = jax.random.permutation(key_rest, others)[:NBR - CAP]
    picked = jnp.concatenate([jnp.full((CAP,), leading, jnp.int32), remaining])
    per_slot = shift_table[jax.random.permutation(key_slots, picked)]
    orders = jax.vmap(permute_slots)(jax.random.split(key_sim, N_GX))
    source = jnp.arange(N_GX, dtype=jnp.int32)[:, None]
    owner_index = (source + per_slot[orders]) % N_GX
    return (owner_index * NBR + orders).reshape(N_GX * NBR)


def draw_brick_home(key, part):
    key = jax.random.fold_in(key, 23)
    group_keys = jax.random.split(key, N_GY * N_GZ)
    homes_all = jax.vmap(group_homes)(group_keys).reshape(N_GY, N_GZ, BRICKS)
    return jnp.transpose(homes_all, (2, 0, 1)).astype(jnp.int32)


def set_ends(drawn, own_key, low, largest):
    index_at = [jax.random.randint(jax.random.fold_in(own_key, axis), (), 0, length) for axis, length in enumerate(drawn.shape)]
    longest = drawn.shape.index(max(drawn.shape))
    neighbour = index_at[:longest] + [(index_at[longest] + 1) % drawn.shape[longest]] + index_at[longest + 1:]
    return drawn.at[tuple(index_at)].set(low).at[tuple(neighbour)].set(largest)


def setup_inputs(seed: int = 0) -> dict:
    arg_keys = jax.random.split(jax.random.key(seed), 4)
    sim_density = draw_sim_density(jax.random.fold_in(arg_keys[3], 71), 0)
    brick_home = draw_brick_home(jax.random.fold_in(arg_keys[3], 71), 0)
    jitter = set_ends(jax.random.randint(arg_keys[2], (NX, NY), 0, STRIDE), jax.random.fold_in(arg_keys[2], 1), 0, STRIDE - 1).astype(jnp.int32)
    return dict(sim_density=sim_density, brick_home=brick_home, jitter=jitter)


GLOW = 5.0
DEPTH_GAIN = 12.0


def pool_pixels(field):
    return field.reshape(field.shape[0] // PIXEL, PIXEL, field.shape[1] // PIXEL, PIXEL).mean(axis=(1, 3))


def reference(sim_density, brick_home, jitter):
    absorb = DEPTH_GAIN / NCOL
    images = []
    for band_y in range(N_GY):
        layers = []
        for layer_z in range(N_GZ):
            block_part = sim_density[:, :, band_y * CY:(band_y + 1) * CY, layer_z * CZ:(layer_z + 1) * CZ]
            inverse = jnp.argsort(brick_home[:, band_y, layer_z]).astype(jnp.int32)
            layers.append(block_part[inverse])
        spatial = jnp.concatenate(layers, axis=3).reshape(NX, CY, NZ)
        tile_peak = spatial.reshape(NX // MT, MT, CY // MT, MT, NZ).max(axis=(1, 3, 4))
        majorant = jnp.repeat(jnp.repeat(tile_peak, MT, axis=0), MT, axis=1).reshape(NX * CY)
        offsets = jitter[:, band_y * CY:(band_y + 1) * CY].reshape(NX * CY, 1, 1).astype(jnp.int32)
        where_at = jnp.broadcast_to(offsets, (NX * CY, NCOL, 1))
        samples = jnp.take_along_axis(spatial.reshape(NX * CY, NCOL, STRIDE), where_at, axis=2)[:, :, 0].T
        ratios = absorb * samples / majorant
        keeping = 1.0 - ratios
        through = jnp.cumprod(keeping, axis=0)
        shading = jnp.concatenate([jnp.ones_like(keeping[:1]), through[:-1]], axis=0)
        radiance = jnp.sum(shading * ratios * (GLOW * samples), axis=0).reshape(NX, CY)
        opacity = (1.0 - through[-1]).reshape(NX, CY)
        images.append(jnp.stack([pool_pixels(radiance), pool_pixels(opacity)]))
    return jnp.concatenate(images, axis=2)
```

```python
import jax
import jax.numpy as jnp
from jax import lax
from jax.experimental import pallas as pl
from jax.experimental.pallas import tpu as pltpu
from jax.sharding import PartitionSpec as P

STRIDE = 16
MT = 8
PIXEL = 4
GLOW = 5.0
DEPTH_GAIN = 12.0

BRICKS = 8
ROWS = 32
QUARTERS = 4
CAP = 2
GROUP = 16
LAYERS = 4
NONE = BRICKS

EXCHANGES = ((2, 2, 1), (1, 1, 1), (2, 2, 0), (1, 1, 0))


def partner_of(position, exchange):
    distance, bit, up = exchange
    goes_up = ((position // bit) % 2) == up
    if isinstance(position, int):
        return (position + (distance if goes_up else -distance)) % GROUP
    step = jnp.where(goes_up, distance, GROUP - distance)
    return lax.rem(position + step, GROUP)


def find_bricks(home_ref, target):
    first = jnp.int32(NONE)
    second = jnp.int32(NONE)
    for brick in range(BRICKS - 1, -1, -1):
        hit = (home_ref[brick] >> 3) == target
        second = jnp.where(hit, first, second)
        first = jnp.where(hit, jnp.int32(brick), first)
    return first, second


def slot_label(home_ref, brick):
    held = home_ref[jnp.minimum(brick, BRICKS - 1)] & (BRICKS - 1)
    return jnp.where(brick < BRICKS, held, NONE)


def pack_kernel(home_ref, dens_ref, *refs):
    outs, sems = refs[: len(EXCHANGES)], refs[len(EXCHANGES)]
    position = lax.axis_index("gx")
    row = lax.broadcasted_iota(jnp.int32, (8, 128), 0)
    copies = []
    for number, exchange in enumerate(EXCHANGES):
        target = partner_of(position, exchange)
        bricks = find_bricks(home_ref, target)
        for place, brick in enumerate(bricks):
            copy = pltpu.make_async_copy(
                dens_ref.at[jnp.minimum(brick, BRICKS - 1)],
                outs[number].at[pl.ds(place * ROWS, ROWS)],
                sems.at[number, place],
            )
            copies.append(copy)
            copy.start()
        labels = [slot_label(home_ref, brick) for brick in bricks]
        outs[number][CAP * ROWS] = jnp.where(row == 0, labels[0], labels[1]).astype(jnp.float32)
    for copy in copies:
        copy.wait()


def select_kernel(home_ref, jitter_ref, dens_ref, *refs):
    arrived = refs[: len(EXCHANGES)]
    out_ref, own_ref, sample_ref, peak_ref, sems = refs[len(EXCHANGES) :]
    position = lax.axis_index("gx")
    own_bricks = find_bricks(home_ref, position)
    copies = []
    for place, brick in enumerate(own_bricks):
        copy = pltpu.make_async_copy(
            dens_ref.at[jnp.minimum(brick, BRICKS - 1)],
            own_ref.at[pl.ds(place * ROWS, ROWS)],
            sems.at[place],
        )
        copy.start()
        copies.append(copy)
    lane = lax.broadcasted_iota(jnp.int32, (8, 128), 1)
    plane = (lane >> 3) & 7
    collision = (lane & 7) * STRIDE
    jitter = jnp.concatenate([jitter_ref[...], jitter_ref[...]], axis=1)

    def handle(source_ref, place, slot):
        @pl.when(slot < BRICKS)
        def _():
            for quarter in range(QUARTERS):
                moved = jnp.take_along_axis(
                    jitter[quarter * 8 : (quarter + 1) * 8],
                    slot * 8 + plane,
                    axis=1,
                    mode="promise_in_bounds",
                )
                where_at = collision + moved
                samples = None
                peak = None
                for x in range(8):
                    cells = source_ref[place * ROWS + x * QUARTERS + quarter]
                    taken = jnp.take_along_axis(cells, where_at, axis=1, mode="promise_in_bounds")
                    samples = taken if x == 0 else jnp.where(plane == x, taken, samples)
                    peak = cells if x == 0 else jnp.maximum(peak, cells)
                sample_ref[slot, quarter] = samples
                peak_ref[quarter, pl.ds(slot, 1), :] = jnp.max(peak, axis=0, keepdims=True)

    for source_ref in arrived:
        for place in range(CAP):
            label = source_ref[CAP * ROWS, place : place + 1, 0:1][0, 0]
            handle(source_ref, place, label.astype(jnp.int32))
    for place in range(CAP):
        copies[place].wait()
        handle(own_ref, place, slot_label(home_ref, own_bricks[place]))
    for quarter in range(QUARTERS):
        for tile in range(BRICKS // 2):
            out_ref[quarter, tile] = jnp.where(
                lane < 64, sample_ref[2 * tile, quarter], sample_ref[2 * tile + 1, quarter]
            )
        peak = jnp.max(peak_ref[quarter], axis=1, keepdims=True)
        out_ref[quarter, BRICKS // 2] = jnp.broadcast_to(peak, (8, 128))


def render_kernel(own_ref, *refs):
    others = refs[: LAYERS - 1]
    out_ref, held_ref = refs[LAYERS - 1 :]
    layer = lax.axis_index("gz")
    held_ref[layer] = own_ref[layer]
    for number, other in enumerate(others):
        held_ref[layer ^ (number + 1)] = other[...]
    lane = lax.broadcasted_iota(jnp.int32, (8, 128), 1)
    tiles = BRICKS // 2
    peak = held_ref[0, tiles]
    for depth in range(1, LAYERS):
        peak = jnp.maximum(peak, held_ref[depth, tiles])
    absorb = jnp.float32(DEPTH_GAIN / (8 * LAYERS))
    light = jnp.zeros((8, 128), jnp.float32)
    cover = jnp.zeros((8, 128), jnp.float32)
    picked = (lane & 3) * 32
    for tile in range(tiles):
        majorant = jnp.where(lane < 64, peak[2 * tile : 2 * tile + 1], peak[2 * tile + 1 : 2 * tile + 2])
        through = None
        radiance = None
        for depth in range(LAYERS):
            samples = held_ref[depth, tile]
            ratio = absorb * samples / majorant
            passed = 1.0 - ratio
            shone = ratio * (GLOW * samples)
            for span in (1, 2, 4):
                shone = shone + passed * pltpu.roll(shone, 128 - span, 1)
                passed = passed * pltpu.roll(passed, 128 - span, 1)
            if depth == 0:
                through, radiance = passed, shone
            else:
                radiance = radiance + through * shone
                through = through * passed
        opacity = 1.0 - through
        pooled = []
        for field in (radiance, opacity):
            field = field + pltpu.roll(field, 120, 1)
            field = field + pltpu.roll(field, 112, 1)
            field = field + pltpu.roll(field, 7, 0)
            field = field + pltpu.roll(field, 6, 0)
            pooled.append(jnp.take_along_axis(field, picked, axis=1, mode="promise_in_bounds"))
        here = (lane >> 2) == tile
        light = jnp.where(here, pooled[0], light)
        cover = jnp.where(here, pooled[1], cover)
    scale = jnp.float32(1.0 / (PIXEL * PIXEL))
    for number, field in enumerate((light, cover)):
        for pixel in range(8 // PIXEL):
            out_ref[number, pixel : pixel + 1, :] = field[pixel * PIXEL : pixel * PIXEL + 1, :16] * scale


def shards(sim_density, brick_home, jitter):
    home = brick_home.reshape(BRICKS)
    density = sim_density.reshape(BRICKS, ROWS, 8, 128)
    smem = pl.BlockSpec(memory_space=pltpu.SMEM)
    vmem = pl.BlockSpec(memory_space=pltpu.VMEM)
    anywhere = pl.BlockSpec(memory_space=pl.ANY)
    box = jax.ShapeDtypeStruct((CAP * ROWS + 1, 8, 128), jnp.float32)
    count = len(EXCHANGES)
    packed = pl.pallas_call(
        pack_kernel,
        out_shape=[box] * count,
        in_specs=[smem, anywhere],
        out_specs=[vmem] * count,
        scratch_shapes=[pltpu.SemaphoreType.DMA((count, CAP))],
        name="pack",
    )(home, density)
    arrived = []
    for exchange, bricks in zip(EXCHANGES, packed):
        pairs = [(source, partner_of(source, exchange)) for source in range(GROUP)]
        arrived.append(lax.ppermute(bricks, "gx", pairs))
    message = pl.pallas_call(
        select_kernel,
        out_shape=jax.ShapeDtypeStruct((QUARTERS, BRICKS // 2 + 1, 8, 128), jnp.float32),
        in_specs=[smem, vmem, anywhere] + [vmem] * count,
        out_specs=vmem,
        scratch_shapes=[
            pltpu.VMEM((CAP * ROWS, 8, 128), jnp.float32),
            pltpu.VMEM((BRICKS, QUARTERS, 8, 128), jnp.float32),
            pltpu.VMEM((QUARTERS, BRICKS, 128), jnp.float32),
            pltpu.SemaphoreType.DMA((CAP,)),
        ],
        name="select",
    )(home, jitter.T, density, *arrived)
    layer = lax.axis_index("gz")
    others = []
    for mask in range(1, LAYERS):
        sent = lax.dynamic_index_in_dim(message, layer ^ mask, 0, keepdims=False)
        others.append(lax.ppermute(sent, "gz", [(source, source ^ mask) for source in range(LAYERS)]))
    image = pl.pallas_call(
        render_kernel,
        out_shape=jax.ShapeDtypeStruct((2, 8 // PIXEL, 16), jnp.float32),
        in_specs=[vmem] * LAYERS,
        out_specs=vmem,
        scratch_shapes=[pltpu.VMEM((LAYERS, BRICKS // 2 + 1, 8, 128), jnp.float32)],
        name="render",
    )(message, *others)
    return jnp.transpose(image, (0, 2, 1))


def solution(mesh):
    in_specs = (P("gx", None, "gy", "gz"), P("gx", "gy", "gz"), P("gx", "gy"))
    out_specs = P(None, "gx", ("gy", "gz"))
    return jax.shard_map(shards, mesh=mesh, in_specs=in_specs, out_specs=out_specs, check_vma=False)
```

```python
import jax
import jax.numpy as jnp
from jax import lax
from jax.experimental import pallas as pl
from jax.experimental.pallas import tpu as pltpu
from jax.sharding import PartitionSpec as P

STRIDE = 16
MT = 8
PIXEL = 4
GLOW = 5.0
DEPTH_GAIN = 12.0

BRICKS = 8
ROWS = 32
QUARTERS = 4
CAP = 2
GROUP = 16
LAYERS = 4
NONE = BRICKS
VMEM_BYTES = 4 << 20

MOVES = (2, 1, -2, -1)
PLACES = len(MOVES) + 1


def find_bricks(home_ref, target):
    first = jnp.int32(NONE)
    second = jnp.int32(NONE)
    for brick in range(BRICKS - 1, -1, -1):
        hit = (home_ref[brick] >> 3) == target
        second = jnp.where(hit, first, second)
        first = jnp.where(hit, jnp.int32(brick), first)
    return first, second


def slot_label(home_ref, brick):
    held = home_ref[jnp.minimum(brick, BRICKS - 1)] & (BRICKS - 1)
    return jnp.where(brick < BRICKS, held, NONE)


def pack_kernel(home_hbm, dens_hbm, *refs):
    outs = refs[:PLACES]
    home_ref, dens_ref, home_sem, dens_sem = refs[PLACES:]
    home_copy = pltpu.make_async_copy(home_hbm, home_ref, home_sem)
    home_copy.start()
    dens_copy = pltpu.make_async_copy(dens_hbm, dens_ref, dens_sem)
    dens_copy.start()
    position = lax.axis_index("gx")
    row = lax.broadcasted_iota(jnp.int32, (8, 128), 0)
    home_copy.wait()
    chosen = []
    for move, out_ref in zip(MOVES + (0,), outs):
        bricks = find_bricks(home_ref, lax.rem(position + (move + GROUP), GROUP))
        labels = [slot_label(home_ref, brick) for brick in bricks]
        out_ref[CAP * ROWS] = jnp.where(row == 0, labels[0], labels[1]).astype(jnp.float32)
        chosen.append([jnp.minimum(brick, BRICKS - 1) for brick in bricks])
    dens_copy.wait()
    for out_ref, bricks in zip(outs, chosen):
        for place, brick in enumerate(bricks):
            out_ref[pl.ds(place * ROWS, ROWS)] = dens_ref[brick]


def select_kernel(jitter_ref, *refs):
    arrived = refs[:PLACES]
    outs = refs[PLACES : PLACES + LAYERS]
    sample_ref, peak_ref = refs[PLACES + LAYERS :]
    layer = lax.axis_index("gz")
    lane = lax.broadcasted_iota(jnp.int32, (8, 128), 1)
    plane = (lane >> 3) & 7
    collision = (lane & 7) * STRIDE
    jitter = jnp.concatenate([jitter_ref[...], jitter_ref[...]], axis=1)

    def handle(source_ref, place):
        label = source_ref[CAP * ROWS, place : place + 1, 0:1][0, 0]
        slot = label.astype(jnp.int32)

        @pl.when(slot < BRICKS)
        def _():
            for quarter in range(QUARTERS):
                moved = jnp.take_along_axis(
                    jitter[quarter * 8 : (quarter + 1) * 8],
                    slot * 8 + plane,
                    axis=1,
                    mode="promise_in_bounds",
                )
                where_at = collision + moved
                samples = None
                peak = None
                for x in range(8):
                    cells = source_ref[place * ROWS + x * QUARTERS + quarter]
                    taken = jnp.take_along_axis(cells, where_at, axis=1, mode="promise_in_bounds")
                    samples = taken if x == 0 else jnp.where(plane == x, taken, samples)
                    peak = cells if x == 0 else jnp.maximum(peak, cells)
                sample_ref[slot, quarter] = samples
                peak_ref[quarter, pl.ds(slot, 1), :] = jnp.max(peak, axis=0, keepdims=True)

    for source_ref in arrived:
        for place in range(CAP):
            handle(source_ref, place)
    for mask, out_ref in enumerate(outs):
        quarter = layer ^ mask
        for tile in range(BRICKS // 2):
            out_ref[tile] = jnp.where(
                lane < 64, sample_ref[2 * tile, quarter], sample_ref[2 * tile + 1, quarter]
            )
        peak = jnp.max(peak_ref[quarter], axis=1, keepdims=True)
        out_ref[BRICKS // 2] = jnp.broadcast_to(peak, (8, 128))


def render_kernel(*refs):
    out_ref, held_ref = refs[LAYERS:]
    layer = lax.axis_index("gz")
    for mask, message in enumerate(refs[:LAYERS]):
        held_ref[layer ^ mask] = message[...]
    lane = lax.broadcasted_iota(jnp.int32, (8, 128), 1)
    tiles = BRICKS // 2
    peak = held_ref[0, tiles]
    for depth in range(1, LAYERS):
        peak = jnp.maximum(peak, held_ref[depth, tiles])
    absorb = jnp.float32(DEPTH_GAIN / (8 * LAYERS))
    light = jnp.zeros((8, 128), jnp.float32)
    cover = jnp.zeros((8, 128), jnp.float32)
    picked = (lane & 3) * 32
    for tile in range(tiles):
        majorant = jnp.where(lane < 64, peak[2 * tile : 2 * tile + 1], peak[2 * tile + 1 : 2 * tile + 2])
        through = None
        radiance = None
        for depth in range(LAYERS):
            samples = held_ref[depth, tile]
            ratio = absorb * samples / majorant
            passed = 1.0 - ratio
            shone = ratio * (GLOW * samples)
            for span in (1, 2, 4):
                shone = shone + passed * pltpu.roll(shone, 128 - span, 1)
                passed = passed * pltpu.roll(passed, 128 - span, 1)
            if depth == 0:
                through, radiance = passed, shone
            else:
                radiance = radiance + through * shone
                through = through * passed
        opacity = 1.0 - through
        pooled = []
        for field in (radiance, opacity):
            field = field + pltpu.roll(field, 120, 1)
            field = field + pltpu.roll(field, 112, 1)
            field = field + pltpu.roll(field, 7, 0)
            field = field + pltpu.roll(field, 6, 0)
            pooled.append(jnp.take_along_axis(field, picked, axis=1, mode="promise_in_bounds"))
        here = (lane >> 2) == tile
        light = jnp.where(here, pooled[0], light)
        cover = jnp.where(here, pooled[1], cover)
    scale = jnp.float32(1.0 / (PIXEL * PIXEL))
    for number, field in enumerate((light, cover)):
        for pixel in range(8 // PIXEL):
            out_ref[number, pixel : pixel + 1, :] = field[pixel * PIXEL : pixel * PIXEL + 1, :16] * scale


def shards(sim_density, brick_home, jitter):
    home = brick_home.reshape(BRICKS)
    density = sim_density.reshape(BRICKS, ROWS, 8, 128)
    vmem = pl.BlockSpec(memory_space=pltpu.VMEM)
    hbm = pl.BlockSpec(memory_space=pltpu.HBM)
    box = jax.ShapeDtypeStruct((CAP * ROWS + 1, 8, 128), jnp.float32)
    packed = pl.pallas_call(
        pack_kernel,
        out_shape=[box] * PLACES,
        in_specs=[hbm, hbm],
        out_specs=[vmem] * PLACES,
        scratch_shapes=[
            pltpu.SMEM((BRICKS,), jnp.int32),
            pltpu.VMEM((BRICKS, ROWS, 8, 128), jnp.float32),
            pltpu.SemaphoreType.DMA,
            pltpu.SemaphoreType.DMA,
        ],
        compiler_params=pltpu.CompilerParams(vmem_limit_bytes=VMEM_BYTES),
        name="pack",
    )(home, density)
    arrived = []
    for move, bricks in zip(MOVES, packed):
        pairs = [(source, (source + move) % GROUP) for source in range(GROUP)]
        arrived.append(lax.ppermute(bricks, "gx", pairs))
    messages = pl.pallas_call(
        select_kernel,
        out_shape=[jax.ShapeDtypeStruct((BRICKS // 2 + 1, 8, 128), jnp.float32)] * LAYERS,
        in_specs=[vmem] * (1 + PLACES),
        out_specs=[vmem] * LAYERS,
        scratch_shapes=[
            pltpu.VMEM((BRICKS, QUARTERS, 8, 128), jnp.float32),
            pltpu.VMEM((QUARTERS, BRICKS, 128), jnp.float32),
        ],
        compiler_params=pltpu.CompilerParams(vmem_limit_bytes=VMEM_BYTES),
        name="select",
    )(jitter.T, packed[-1], *arrived)
    others = []
    for mask in range(1, LAYERS):
        pairs = [(source, source ^ mask) for source in range(LAYERS)]
        others.append(lax.ppermute(messages[mask], "gz", pairs))
    image = pl.pallas_call(
        render_kernel,
        out_shape=jax.ShapeDtypeStruct((2, 8 // PIXEL, 16), jnp.float32),
        in_specs=[vmem] * LAYERS,
        out_specs=vmem,
        scratch_shapes=[pltpu.VMEM((LAYERS, BRICKS // 2 + 1, 8, 128), jnp.float32)],
        compiler_params=pltpu.CompilerParams(vmem_limit_bytes=VMEM_BYTES),
        name="render",
    )(messages[0], *others)
    return jnp.transpose(image, (0, 2, 1))


def solution(mesh):
    in_specs = (P("gx", None, "gy", "gz"), P("gx", "gy", "gz"), P("gx", "gy"))
    out_specs = P(None, "gx", ("gy", "gz"))
    return jax.shard_map(shards, mesh=mesh, in_specs=in_specs, out_specs=out_specs, check_vma=False)
```

```python
import jax
import jax.numpy as jnp
from jax import lax
from jax.experimental import pallas as pl
from jax.experimental.pallas import tpu as pltpu
from jax.sharding import PartitionSpec as P

STRIDE = 16
MT = 8
PIXEL = 4
GLOW = 5.0
DEPTH_GAIN = 12.0

BRICKS = 8
ROWS = 32
QUARTERS = 4
CAP = 2
GROUP = 16
LAYERS = 4
NONE = BRICKS
VMEM_BYTES = 4 << 20

MOVES = (1, 2, -2, -1)
EARLY = 2
PLACES = len(MOVES) + 1
SENDS = ((3, 2, 0, 1), (2, 3, 1, 0), (1, 0, 3, 2))
TILES = BRICKS // 2


def look_up(table, position):
    packed = sum(entry << (4 * index) for index, entry in enumerate(table))
    return (jnp.int32(packed) >> (4 * position)) & 15


def find_bricks(home_ref, target):
    first = jnp.int32(NONE)
    second = jnp.int32(NONE)
    for brick in range(BRICKS - 1, -1, -1):
        hit = (home_ref[brick] >> 3) == target
        second = jnp.where(hit, first, second)
        first = jnp.where(hit, jnp.int32(brick), first)
    return first, second


def slot_label(home_ref, brick):
    held = home_ref[jnp.minimum(brick, BRICKS - 1)] & (BRICKS - 1)
    return jnp.where(brick < BRICKS, held, NONE)


def pack_kernel(home_hbm, dens_hbm, *refs):
    outs = refs[:PLACES]
    home_ref, dens_ref, home_sem, dens_sem = refs[PLACES:]
    home_copy = pltpu.make_async_copy(home_hbm, home_ref, home_sem)
    home_copy.start()
    dens_copy = pltpu.make_async_copy(dens_hbm, dens_ref, dens_sem)
    dens_copy.start()
    position = lax.axis_index("gx")
    row = lax.broadcasted_iota(jnp.int32, (8, 128), 0)
    home_copy.wait()
    chosen = []
    for move, out_ref in zip(MOVES + (0,), outs):
        bricks = find_bricks(home_ref, lax.rem(position + (move + GROUP), GROUP))
        labels = [slot_label(home_ref, brick) for brick in bricks]
        out_ref[CAP * ROWS] = jnp.where(row == 0, labels[0], labels[1]).astype(jnp.float32)
        chosen.append([jnp.minimum(brick, BRICKS - 1) for brick in bricks])
    dens_copy.wait()
    for out_ref, bricks in zip(outs, chosen):
        for place, brick in enumerate(bricks):
            out_ref[pl.ds(place * ROWS, ROWS)] = dens_ref[brick]


def take_samples(jitter_ref, arrived, sample_ref, peak_ref):
    lane = lax.broadcasted_iota(jnp.int32, (8, 128), 1)
    plane = (lane >> 3) & 7
    collision = (lane & 7) * STRIDE
    jitter = jnp.concatenate([jitter_ref[...], jitter_ref[...]], axis=1)
    slots = []
    for source_ref in arrived:
        for place in range(CAP):
            label = source_ref[CAP * ROWS, place : place + 1, 0:1][0, 0]
            slots.append(label.astype(jnp.int32))
    for number, slot in enumerate(slots):
        source_ref, place = arrived[number // CAP], number % CAP
        for quarter in range(QUARTERS):
            moved = jnp.take_along_axis(
                jitter[quarter * 8 : (quarter + 1) * 8],
                slot * 8 + plane,
                axis=1,
                mode="promise_in_bounds",
            )
            where_at = collision + moved
            samples = None
            peak = None
            for x in range(8):
                cells = source_ref[place * ROWS + x * QUARTERS + quarter]
                taken = jnp.take_along_axis(cells, where_at, axis=1, mode="promise_in_bounds")
                samples = taken if x == 0 else jnp.where(plane == x, taken, samples)
                peak = cells if x == 0 else jnp.maximum(peak, cells)
            sample_ref[slot, quarter] = samples
            peak_ref[quarter, pl.ds(slot, 1), :] = jnp.max(peak, axis=0, keepdims=True)


def early_kernel(jitter_ref, *refs):
    arrived = refs[: EARLY + 1]
    sample_ref, peak_ref = refs[EARLY + 1 :]
    take_samples(jitter_ref, arrived, sample_ref, peak_ref)


def late_kernel(jitter_ref, early_samples, early_peaks, *refs):
    count = len(MOVES) - EARLY
    arrived = refs[:count]
    outs = refs[count : count + LAYERS]
    sample_ref, peak_ref = refs[count + LAYERS :]
    sample_ref[...] = early_samples[...]
    peak_ref[...] = early_peaks[...]
    take_samples(jitter_ref, arrived, sample_ref, peak_ref)
    layer = lax.axis_index("gz")
    lane = lax.broadcasted_iota(jnp.int32, (8, 128), 1)
    quarters = [layer] + [look_up(table, layer) for table in SENDS]
    for quarter, out_ref in zip(quarters, outs):
        for tile in range(TILES):
            out_ref[tile] = jnp.where(
                lane < 64, sample_ref[2 * tile, quarter], sample_ref[2 * tile + 1, quarter]
            )
        peak = jnp.max(peak_ref[quarter, :BRICKS], axis=1, keepdims=True)
        out_ref[TILES] = jnp.broadcast_to(peak, (8, 128))


def render_kernel(*refs):
    out_ref, held_ref = refs[LAYERS:]
    layer = lax.axis_index("gz")
    sources = [layer]
    for table in SENDS:
        sources.append(look_up([table.index(place) for place in range(LAYERS)], layer))
    for source, message in zip(sources, refs[:LAYERS]):
        held_ref[source] = message[...]
    lane = lax.broadcasted_iota(jnp.int32, (8, 128), 1)
    tiles = TILES
    peak = held_ref[0, tiles]
    for depth in range(1, LAYERS):
        peak = jnp.maximum(peak, held_ref[depth, tiles])
    absorb = jnp.float32(DEPTH_GAIN / (8 * LAYERS))
    light = jnp.zeros((8, 128), jnp.float32)
    cover = jnp.zeros((8, 128), jnp.float32)
    picked = (lane & 3) * 32
    for tile in range(tiles):
        majorant = jnp.where(lane < 64, peak[2 * tile : 2 * tile + 1], peak[2 * tile + 1 : 2 * tile + 2])
        through = None
        radiance = None
        for depth in range(LAYERS):
            samples = held_ref[depth, tile]
            ratio = absorb * samples / majorant
            passed = 1.0 - ratio
            shone = ratio * (GLOW * samples)
            for span in (1, 2, 4):
                shone = shone + passed * pltpu.roll(shone, 128 - span, 1)
                passed = passed * pltpu.roll(passed, 128 - span, 1)
            if depth == 0:
                through, radiance = passed, shone
            else:
                radiance = radiance + through * shone
                through = through * passed
        opacity = 1.0 - through
        pooled = []
        for field in (radiance, opacity):
            field = field + pltpu.roll(field, 120, 1)
            field = field + pltpu.roll(field, 112, 1)
            field = field + pltpu.roll(field, 7, 0)
            field = field + pltpu.roll(field, 6, 0)
            pooled.append(jnp.take_along_axis(field, picked, axis=1, mode="promise_in_bounds"))
        here = (lane >> 2) == tile
        light = jnp.where(here, pooled[0], light)
        cover = jnp.where(here, pooled[1], cover)
    scale = jnp.float32(1.0 / (PIXEL * PIXEL))
    for number, field in enumerate((light, cover)):
        for pixel in range(8 // PIXEL):
            out_ref[number, pixel : pixel + 1, :] = field[pixel * PIXEL : pixel * PIXEL + 1, :16] * scale


def shards(sim_density, brick_home, jitter):
    home = pltpu.with_memory_space_constraint(brick_home.reshape(BRICKS), pltpu.HBM)
    density = pltpu.with_memory_space_constraint(
        sim_density.reshape(BRICKS, ROWS, 8, 128), pltpu.HBM
    )
    vmem = pl.BlockSpec(memory_space=pltpu.VMEM)
    hbm = pl.BlockSpec(memory_space=pltpu.HBM)
    params = pltpu.CompilerParams(vmem_limit_bytes=VMEM_BYTES)
    box = jax.ShapeDtypeStruct((CAP * ROWS + 1, 8, 128), jnp.float32)
    packed = pl.pallas_call(
        pack_kernel,
        out_shape=[box] * PLACES,
        in_specs=[hbm, hbm],
        out_specs=[vmem] * PLACES,
        scratch_shapes=[
            pltpu.SMEM((BRICKS,), jnp.int32),
            pltpu.VMEM((BRICKS, ROWS, 8, 128), jnp.float32),
            pltpu.SemaphoreType.DMA,
            pltpu.SemaphoreType.DMA,
        ],
        compiler_params=params,
        name="pack",
    )(home, density)
    arrived = []
    for move, bricks in zip(MOVES, packed):
        pairs = [(source, (source + move) % GROUP) for source in range(GROUP)]
        arrived.append(lax.ppermute(bricks, "gx", pairs))
    sample_box = (BRICKS + 1, QUARTERS, 8, 128)
    peak_box = (QUARTERS, 2 * BRICKS, 128)
    gathered = pl.pallas_call(
        early_kernel,
        out_shape=[
            jax.ShapeDtypeStruct(sample_box, jnp.float32),
            jax.ShapeDtypeStruct(peak_box, jnp.float32),
        ],
        in_specs=[vmem] * (2 + EARLY),
        out_specs=[vmem] * 2,
        compiler_params=params,
        name="early",
    )(jitter.T, packed[-1], *arrived[:EARLY])
    messages = pl.pallas_call(
        late_kernel,
        out_shape=[jax.ShapeDtypeStruct((TILES + 1, 8, 128), jnp.float32)] * LAYERS,
        in_specs=[vmem] * (3 + len(MOVES) - EARLY),
        out_specs=[vmem] * LAYERS,
        scratch_shapes=[
            pltpu.VMEM(sample_box, jnp.float32),
            pltpu.VMEM(peak_box, jnp.float32),
        ],
        compiler_params=params,
        name="late",
    )(jitter.T, *gathered, *arrived[EARLY:])
    others = []
    for table, message in zip(SENDS, messages[1:]):
        others.append(lax.ppermute(message, "gz", list(enumerate(table))))
    image = pl.pallas_call(
        render_kernel,
        out_shape=jax.ShapeDtypeStruct((2, 8 // PIXEL, 16), jnp.float32),
        in_specs=[vmem] * LAYERS,
        out_specs=vmem,
        scratch_shapes=[pltpu.VMEM((LAYERS, TILES + 1, 8, 128), jnp.float32)],
        compiler_params=params,
        name="render",
    )(messages[0], *others)
    return jnp.transpose(image, (0, 2, 1))


def solution(mesh):
    in_specs = (P("gx", None, "gy", "gz"), P("gx", "gy", "gz"), P("gx", "gy"))
    out_specs = P(None, "gx", ("gy", "gz"))
    return jax.shard_map(shards, mesh=mesh, in_specs=in_specs, out_specs=out_specs, check_vma=False)
```

```python
import jax
import jax.numpy as jnp
from jax import lax
from jax.experimental import pallas as pl
from jax.experimental.pallas import tpu as pltpu
from jax.sharding import PartitionSpec as P

STRIDE = 16
MT = 8
PIXEL = 4
GLOW = 5.0
DEPTH_GAIN = 12.0

BRICKS = 8
ROWS = 32
QUARTERS = 4
CAP = 2
GROUP = 16
LAYERS = 4
NONE = BRICKS
VMEM_BYTES = 4 << 20

MOVES = (1, 2, -2, -1)
EARLY = (0, 2)
LATE = (1, 3)
PLACES = len(MOVES) + 1
SENDS = ((3, 2, 0, 1), (2, 3, 1, 0), (1, 0, 3, 2))
TILES = BRICKS // 2


def look_up(table, position):
    packed = sum(entry << (4 * index) for index, entry in enumerate(table))
    return (jnp.int32(packed) >> (4 * position)) & 15


def find_bricks(home_ref, target):
    first = jnp.int32(NONE)
    second = jnp.int32(NONE)
    for brick in range(BRICKS - 1, -1, -1):
        hit = (home_ref[brick] >> 3) == target
        second = jnp.where(hit, first, second)
        first = jnp.where(hit, jnp.int32(brick), first)
    return first, second


def slot_label(home_ref, brick):
    held = home_ref[jnp.minimum(brick, BRICKS - 1)] & (BRICKS - 1)
    return jnp.where(brick < BRICKS, held, NONE)


def pack_kernel(home_hbm, dens_hbm, *refs):
    outs = refs[:PLACES]
    home_ref, dens_ref, home_sem, dens_sem = refs[PLACES:]
    home_copy = pltpu.make_async_copy(home_hbm, home_ref, home_sem)
    home_copy.start()
    dens_copy = pltpu.make_async_copy(dens_hbm, dens_ref, dens_sem)
    dens_copy.start()
    position = lax.axis_index("gx")
    row = lax.broadcasted_iota(jnp.int32, (8, 128), 0)
    home_copy.wait()
    chosen = []
    for move, out_ref in zip(MOVES + (0,), outs):
        bricks = find_bricks(home_ref, lax.rem(position + (move + GROUP), GROUP))
        labels = [slot_label(home_ref, brick) for brick in bricks]
        out_ref[CAP * ROWS] = jnp.where(row == 0, labels[0], labels[1]).astype(jnp.float32)
        chosen.append([jnp.minimum(brick, BRICKS - 1) for brick in bricks])
    dens_copy.wait()
    for out_ref, bricks in zip(outs, chosen):
        for place, brick in enumerate(bricks):
            out_ref[pl.ds(place * ROWS, ROWS)] = dens_ref[brick]


def take_samples(jitter_ref, arrived, sample_ref, peak_ref):
    lane = lax.broadcasted_iota(jnp.int32, (8, 128), 1)
    plane = (lane >> 3) & 7
    collision = (lane & 7) * STRIDE
    jitter = jnp.concatenate([jitter_ref[...], jitter_ref[...]], axis=1)
    slots = []
    for source_ref in arrived:
        for place in range(CAP):
            label = source_ref[CAP * ROWS, place : place + 1, 0:1][0, 0]
            slots.append(label.astype(jnp.int32))
    for number, slot in enumerate(slots):
        source_ref, place = arrived[number // CAP], number % CAP
        for quarter in range(QUARTERS):
            moved = jnp.take_along_axis(
                jitter[quarter * 8 : (quarter + 1) * 8],
                slot * 8 + plane,
                axis=1,
                mode="promise_in_bounds",
            )
            where_at = collision + moved
            samples = None
            peak = None
            for x in range(8):
                cells = source_ref[place * ROWS + x * QUARTERS + quarter]
                taken = jnp.take_along_axis(cells, where_at, axis=1, mode="promise_in_bounds")
                samples = taken if x == 0 else jnp.where(plane == x, taken, samples)
                peak = cells if x == 0 else jnp.maximum(peak, cells)
            sample_ref[slot, quarter] = samples
            peak_ref[quarter, pl.ds(slot, 1), :] = jnp.max(peak, axis=0, keepdims=True)


def early_kernel(jitter_ref, *refs):
    arrived = refs[: len(EARLY) + 1]
    sample_ref, peak_ref = refs[len(EARLY) + 1 :]
    take_samples(jitter_ref, arrived, sample_ref, peak_ref)


def late_kernel(jitter_ref, early_samples, early_peaks, *refs):
    count = len(LATE)
    arrived = refs[:count]
    outs = refs[count : count + LAYERS]
    sample_ref, peak_ref = refs[count + LAYERS :]
    sample_ref[...] = early_samples[...]
    peak_ref[...] = early_peaks[...]
    take_samples(jitter_ref, arrived, sample_ref, peak_ref)
    layer = lax.axis_index("gz")
    lane = lax.broadcasted_iota(jnp.int32, (8, 128), 1)
    quarters = [layer] + [look_up(table, layer) for table in SENDS]
    for quarter, out_ref in zip(quarters, outs):
        for tile in range(TILES):
            out_ref[tile] = jnp.where(
                lane < 64, sample_ref[2 * tile, quarter], sample_ref[2 * tile + 1, quarter]
            )
        peak = jnp.max(peak_ref[quarter, :BRICKS], axis=1, keepdims=True)
        out_ref[TILES] = jnp.broadcast_to(peak, (8, 128))


def render_kernel(*refs):
    out_ref, held_ref = refs[LAYERS:]
    layer = lax.axis_index("gz")
    sources = [layer]
    for table in SENDS:
        sources.append(look_up([table.index(place) for place in range(LAYERS)], layer))
    for source, message in zip(sources, refs[:LAYERS]):
        held_ref[source] = message[...]
    lane = lax.broadcasted_iota(jnp.int32, (8, 128), 1)
    tiles = TILES
    peak = held_ref[0, tiles]
    for depth in range(1, LAYERS):
        peak = jnp.maximum(peak, held_ref[depth, tiles])
    absorb = jnp.float32(DEPTH_GAIN / (8 * LAYERS))
    light = jnp.zeros((8, 128), jnp.float32)
    cover = jnp.zeros((8, 128), jnp.float32)
    picked = (lane & 3) * 32
    for tile in range(tiles):
        majorant = jnp.where(lane < 64, peak[2 * tile : 2 * tile + 1], peak[2 * tile + 1 : 2 * tile + 2])
        through = None
        radiance = None
        for depth in range(LAYERS):
            samples = held_ref[depth, tile]
            ratio = absorb * samples / majorant
            passed = 1.0 - ratio
            shone = ratio * (GLOW * samples)
            for span in (1, 2, 4):
                shone = shone + passed * pltpu.roll(shone, 128 - span, 1)
                passed = passed * pltpu.roll(passed, 128 - span, 1)
            if depth == 0:
                through, radiance = passed, shone
            else:
                radiance = radiance + through * shone
                through = through * passed
        opacity = 1.0 - through
        pooled = []
        for field in (radiance, opacity):
            field = field + pltpu.roll(field, 120, 1)
            field = field + pltpu.roll(field, 112, 1)
            field = field + pltpu.roll(field, 7, 0)
            field = field + pltpu.roll(field, 6, 0)
            pooled.append(jnp.take_along_axis(field, picked, axis=1, mode="promise_in_bounds"))
        here = (lane >> 2) == tile
        light = jnp.where(here, pooled[0], light)
        cover = jnp.where(here, pooled[1], cover)
    scale = jnp.float32(1.0 / (PIXEL * PIXEL))
    for number, field in enumerate((light, cover)):
        for pixel in range(8 // PIXEL):
            out_ref[number, pixel : pixel + 1, :] = field[pixel * PIXEL : pixel * PIXEL + 1, :16] * scale


def shards(sim_density, brick_home, jitter):
    home = pltpu.with_memory_space_constraint(brick_home.reshape(BRICKS), pltpu.HBM)
    density = pltpu.with_memory_space_constraint(
        sim_density.reshape(BRICKS, ROWS, 8, 128), pltpu.HBM
    )
    vmem = pl.BlockSpec(memory_space=pltpu.VMEM)
    hbm = pl.BlockSpec(memory_space=pltpu.HBM)
    params = pltpu.CompilerParams(vmem_limit_bytes=VMEM_BYTES)
    box = jax.ShapeDtypeStruct((CAP * ROWS + 1, 8, 128), jnp.float32)
    packed = pl.pallas_call(
        pack_kernel,
        out_shape=[box] * PLACES,
        in_specs=[hbm, hbm],
        out_specs=[vmem] * PLACES,
        scratch_shapes=[
            pltpu.SMEM((BRICKS,), jnp.int32),
            pltpu.VMEM((BRICKS, ROWS, 8, 128), jnp.float32),
            pltpu.SemaphoreType.DMA,
            pltpu.SemaphoreType.DMA,
        ],
        compiler_params=params,
        name="pack",
    )(home, density)
    arrived = []
    for move, bricks in zip(MOVES, packed):
        pairs = [(source, (source + move) % GROUP) for source in range(GROUP)]
        arrived.append(lax.ppermute(bricks, "gx", pairs))
    sample_box = (BRICKS + 1, QUARTERS, 8, 128)
    peak_box = (QUARTERS, 2 * BRICKS, 128)
    gathered = pl.pallas_call(
        early_kernel,
        out_shape=[
            jax.ShapeDtypeStruct(sample_box, jnp.float32),
            jax.ShapeDtypeStruct(peak_box, jnp.float32),
        ],
        in_specs=[vmem] * (2 + len(EARLY)),
        out_specs=[vmem] * 2,
        compiler_params=params,
        name="early",
    )(jitter.T, packed[-1], *[arrived[number] for number in EARLY])
    messages = pl.pallas_call(
        late_kernel,
        out_shape=[jax.ShapeDtypeStruct((TILES + 1, 8, 128), jnp.float32)] * LAYERS,
        in_specs=[vmem] * (3 + len(LATE)),
        out_specs=[vmem] * LAYERS,
        scratch_shapes=[
            pltpu.VMEM(sample_box, jnp.float32),
            pltpu.VMEM(peak_box, jnp.float32),
        ],
        compiler_params=params,
        name="late",
    )(jitter.T, *gathered, *[arrived[number] for number in LATE])
    others = []
    for table, message in zip(SENDS, messages[1:]):
        others.append(lax.ppermute(message, "gz", list(enumerate(table))))
    image = pl.pallas_call(
        render_kernel,
        out_shape=jax.ShapeDtypeStruct((2, 8 // PIXEL, 16), jnp.float32),
        in_specs=[vmem] * LAYERS,
        out_specs=vmem,
        scratch_shapes=[pltpu.VMEM((LAYERS, TILES + 1, 8, 128), jnp.float32)],
        compiler_params=params,
        name="render",
    )(messages[0], *others)
    return jnp.transpose(image, (0, 2, 1))


def solution(mesh):
    in_specs = (P("gx", None, "gy", "gz"), P("gx", "gy", "gz"), P("gx", "gy"))
    out_specs = P(None, "gx", ("gy", "gz"))
    return jax.shard_map(shards, mesh=mesh, in_specs=in_specs, out_specs=out_specs, check_vma=False)
```

```python
import jax
import jax.numpy as jnp
from jax import lax
from jax.experimental import pallas as pl
from jax.experimental.pallas import tpu as pltpu
from jax.sharding import PartitionSpec as P

STRIDE = 16
MT = 8
PIXEL = 4
GLOW = 5.0
DEPTH_GAIN = 12.0

BRICKS = 8
ROWS = 32
QUARTERS = 4
CAP = 2
GROUP = 16
LAYERS = 4
NONE = BRICKS
VMEM_BYTES = 4 << 20

MOVES = ((1, 1), (2, -2), (-2, 2), (-1, -1))
EARLY = (0, 1)
LATE = (2, 3)
PLACES = len(MOVES) + 1
SENDS = ((3, 2, 0, 1), (2, 3, 1, 0), (1, 0, 3, 2))
TILES = BRICKS // 2


def look_up(table, position):
    packed = sum(entry << (4 * index) for index, entry in enumerate(table))
    return (jnp.int32(packed) >> (4 * position)) & 15


def find_bricks(home_ref, target):
    first = jnp.int32(NONE)
    second = jnp.int32(NONE)
    for brick in range(BRICKS - 1, -1, -1):
        hit = (home_ref[brick] >> 3) == target
        second = jnp.where(hit, first, second)
        first = jnp.where(hit, jnp.int32(brick), first)
    return first, second


def slot_label(home_ref, brick):
    held = home_ref[jnp.minimum(brick, BRICKS - 1)] & (BRICKS - 1)
    return jnp.where(brick < BRICKS, held, NONE)


def pack_kernel(home_hbm, dens_hbm, *refs):
    outs = refs[:PLACES]
    home_ref, dens_ref, home_sem, dens_sem = refs[PLACES:]
    home_copy = pltpu.make_async_copy(home_hbm, home_ref, home_sem)
    home_copy.start()
    dens_copy = pltpu.make_async_copy(dens_hbm, dens_ref, dens_sem)
    dens_copy.start()
    position = lax.axis_index("gx")
    row = lax.broadcasted_iota(jnp.int32, (8, 128), 0)
    home_copy.wait()
    chosen = []
    odd = (position & 1) == 1
    for (step, odd_step), out_ref in zip(MOVES + ((0, 0),), outs):
        target = (position + jnp.where(odd, odd_step, step) + GROUP) & (GROUP - 1)
        bricks = find_bricks(home_ref, target)
        labels = [slot_label(home_ref, brick) for brick in bricks]
        out_ref[CAP * ROWS] = jnp.where(row == 0, labels[0], labels[1]).astype(jnp.float32)
        chosen.append([jnp.minimum(brick, BRICKS - 1) for brick in bricks])
    dens_copy.wait()
    for out_ref, bricks in zip(outs, chosen):
        for place, brick in enumerate(bricks):
            out_ref[pl.ds(place * ROWS, ROWS)] = dens_ref[brick]


def take_samples(jitter_ref, arrived, sample_ref, peak_ref):
    lane = lax.broadcasted_iota(jnp.int32, (8, 128), 1)
    plane = (lane >> 3) & 7
    collision = (lane & 7) * STRIDE
    jitter = jnp.concatenate([jitter_ref[...], jitter_ref[...]], axis=1)
    slots = []
    for source_ref in arrived:
        for place in range(CAP):
            label = source_ref[CAP * ROWS, place : place + 1, 0:1][0, 0]
            slots.append(label.astype(jnp.int32))
    for number, slot in enumerate(slots):
        source_ref, place = arrived[number // CAP], number % CAP
        for quarter in range(QUARTERS):
            moved = jnp.take_along_axis(
                jitter[quarter * 8 : (quarter + 1) * 8],
                slot * 8 + plane,
                axis=1,
                mode="promise_in_bounds",
            )
            where_at = collision + moved
            samples = None
            peak = None
            for x in range(8):
                cells = source_ref[place * ROWS + x * QUARTERS + quarter]
                taken = jnp.take_along_axis(cells, where_at, axis=1, mode="promise_in_bounds")
                samples = taken if x == 0 else jnp.where(plane == x, taken, samples)
                peak = cells if x == 0 else jnp.maximum(peak, cells)
            sample_ref[slot, quarter] = samples
            peak_ref[quarter, pl.ds(slot, 1), :] = jnp.max(peak, axis=0, keepdims=True)


def early_kernel(jitter_ref, *refs):
    arrived = refs[: len(EARLY) + 1]
    sample_ref, peak_ref = refs[len(EARLY) + 1 :]
    take_samples(jitter_ref, arrived, sample_ref, peak_ref)


def late_kernel(jitter_ref, early_samples, early_peaks, *refs):
    count = len(LATE)
    arrived = refs[:count]
    outs = refs[count : count + LAYERS]
    sample_ref, peak_ref = refs[count + LAYERS :]
    sample_ref[...] = early_samples[...]
    peak_ref[...] = early_peaks[...]
    take_samples(jitter_ref, arrived, sample_ref, peak_ref)
    layer = lax.axis_index("gz")
    lane = lax.broadcasted_iota(jnp.int32, (8, 128), 1)
    quarters = [layer] + [look_up(table, layer) for table in SENDS]
    for quarter, out_ref in zip(quarters, outs):
        for tile in range(TILES):
            out_ref[tile] = jnp.where(
                lane < 64, sample_ref[2 * tile, quarter], sample_ref[2 * tile + 1, quarter]
            )
        peak = jnp.max(peak_ref[quarter, :BRICKS], axis=1, keepdims=True)
        out_ref[TILES] = jnp.broadcast_to(peak, (8, 128))


def render_kernel(*refs):
    out_ref, held_ref = refs[LAYERS:]
    layer = lax.axis_index("gz")
    sources = [layer]
    for table in SENDS:
        sources.append(look_up([table.index(place) for place in range(LAYERS)], layer))
    for source, message in zip(sources, refs[:LAYERS]):
        held_ref[source] = message[...]
    lane = lax.broadcasted_iota(jnp.int32, (8, 128), 1)
    tiles = TILES
    peak = held_ref[0, tiles]
    for depth in range(1, LAYERS):
        peak = jnp.maximum(peak, held_ref[depth, tiles])
    absorb = jnp.float32(DEPTH_GAIN / (8 * LAYERS))
    light = jnp.zeros((8, 128), jnp.float32)
    cover = jnp.zeros((8, 128), jnp.float32)
    picked = (lane & 3) * 32
    for tile in range(tiles):
        majorant = jnp.where(lane < 64, peak[2 * tile : 2 * tile + 1], peak[2 * tile + 1 : 2 * tile + 2])
        through = None
        radiance = None
        for depth in range(LAYERS):
            samples = held_ref[depth, tile]
            ratio = absorb * samples / majorant
            passed = 1.0 - ratio
            shone = ratio * (GLOW * samples)
            for span in (1, 2, 4):
                shone = shone + passed * pltpu.roll(shone, 128 - span, 1)
                passed = passed * pltpu.roll(passed, 128 - span, 1)
            if depth == 0:
                through, radiance = passed, shone
            else:
                radiance = radiance + through * shone
                through = through * passed
        opacity = 1.0 - through
        pooled = []
        for field in (radiance, opacity):
            field = field + pltpu.roll(field, 120, 1)
            field = field + pltpu.roll(field, 112, 1)
            field = field + pltpu.roll(field, 7, 0)
            field = field + pltpu.roll(field, 6, 0)
            pooled.append(jnp.take_along_axis(field, picked, axis=1, mode="promise_in_bounds"))
        here = (lane >> 2) == tile
        light = jnp.where(here, pooled[0], light)
        cover = jnp.where(here, pooled[1], cover)
    scale = jnp.float32(1.0 / (PIXEL * PIXEL))
    for number, field in enumerate((light, cover)):
        for pixel in range(8 // PIXEL):
            out_ref[number, pixel : pixel + 1, :] = field[pixel * PIXEL : pixel * PIXEL + 1, :16] * scale


def shards(sim_density, brick_home, jitter):
    home = pltpu.with_memory_space_constraint(brick_home.reshape(BRICKS), pltpu.HBM)
    density = pltpu.with_memory_space_constraint(
        sim_density.reshape(BRICKS, ROWS, 8, 128), pltpu.HBM
    )
    vmem = pl.BlockSpec(memory_space=pltpu.VMEM)
    hbm = pl.BlockSpec(memory_space=pltpu.HBM)
    params = pltpu.CompilerParams(vmem_limit_bytes=VMEM_BYTES)
    box = jax.ShapeDtypeStruct((CAP * ROWS + 1, 8, 128), jnp.float32)
    packed = pl.pallas_call(
        pack_kernel,
        out_shape=[box] * PLACES,
        in_specs=[hbm, hbm],
        out_specs=[vmem] * PLACES,
        scratch_shapes=[
            pltpu.SMEM((BRICKS,), jnp.int32),
            pltpu.VMEM((BRICKS, ROWS, 8, 128), jnp.float32),
            pltpu.SemaphoreType.DMA,
            pltpu.SemaphoreType.DMA,
        ],
        compiler_params=params,
        name="pack",
    )(home, density)
    arrived = []
    for move, bricks in zip(MOVES, packed):
        pairs = [(source, (source + move[source % 2]) % GROUP) for source in range(GROUP)]
        arrived.append(lax.ppermute(bricks, "gx", pairs))
    sample_box = (BRICKS + 1, QUARTERS, 8, 128)
    peak_box = (QUARTERS, 2 * BRICKS, 128)
    gathered = pl.pallas_call(
        early_kernel,
        out_shape=[
            jax.ShapeDtypeStruct(sample_box, jnp.float32),
            jax.ShapeDtypeStruct(peak_box, jnp.float32),
        ],
        in_specs=[vmem] * (2 + len(EARLY)),
        out_specs=[vmem] * 2,
        compiler_params=params,
        name="early",
    )(jitter.T, packed[-1], *[arrived[number] for number in EARLY])
    messages = pl.pallas_call(
        late_kernel,
        out_shape=[jax.ShapeDtypeStruct((TILES + 1, 8, 128), jnp.float32)] * LAYERS,
        in_specs=[vmem] * (3 + len(LATE)),
        out_specs=[vmem] * LAYERS,
        scratch_shapes=[
            pltpu.VMEM(sample_box, jnp.float32),
            pltpu.VMEM(peak_box, jnp.float32),
        ],
        compiler_params=params,
        name="late",
    )(jitter.T, *gathered, *[arrived[number] for number in LATE])
    others = []
    for table, message in zip(SENDS, messages[1:]):
        others.append(lax.ppermute(message, "gz", list(enumerate(table))))
    image = pl.pallas_call(
        render_kernel,
        out_shape=jax.ShapeDtypeStruct((2, 8 // PIXEL, 16), jnp.float32),
        in_specs=[vmem] * LAYERS,
        out_specs=vmem,
        scratch_shapes=[pltpu.VMEM((LAYERS, TILES + 1, 8, 128), jnp.float32)],
        compiler_params=params,
        name="render",
    )(messages[0], *others)
    return jnp.transpose(image, (0, 2, 1))


def solution(mesh):
    in_specs = (P("gx", None, "gy", "gz"), P("gx", "gy", "gz"), P("gx", "gy"))
    out_specs = P(None, "gx", ("gy", "gz"))
    return jax.shard_map(shards, mesh=mesh, in_specs=in_specs, out_specs=out_specs, check_vma=False)
```

```python
import jax
import jax.numpy as jnp
from jax import lax
from jax.experimental import pallas as pl
from jax.experimental.pallas import tpu as pltpu
from jax.sharding import PartitionSpec as P

STRIDE = 16
MT = 8
PIXEL = 4
GLOW = 5.0
DEPTH_GAIN = 12.0

BRICKS = 8
ROWS = 32
QUARTERS = 4
CAP = 2
GROUP = 16
LAYERS = 4
NONE = BRICKS
VMEM_BYTES = 4 << 20

MOVES = ((1, 1), (2, -2), (-2, 2), (-1, -1))
EARLY = (0, 1)
LATE = (2, 3)
PLACES = len(MOVES) + 1
SENDS = ((3, 2, 0, 1), (2, 3, 1, 0), (1, 0, 3, 2))
TILES = BRICKS // 2


def look_up(table, position):
    packed = sum(entry << (4 * index) for index, entry in enumerate(table))
    return (jnp.int32(packed) >> (4 * position)) & 15


def find_bricks(home_ref, target):
    first = jnp.int32(NONE)
    second = jnp.int32(NONE)
    for brick in range(BRICKS - 1, -1, -1):
        hit = (home_ref[brick] >> 3) == target
        second = jnp.where(hit, first, second)
        first = jnp.where(hit, jnp.int32(brick), first)
    return first, second


def slot_label(home_ref, brick):
    held = home_ref[jnp.minimum(brick, BRICKS - 1)] & (BRICKS - 1)
    return jnp.where(brick < BRICKS, held, NONE)


def pack_kernel(home_hbm, dens_hbm, *refs):
    outs = refs[:PLACES]
    home_ref, dens_ref, home_sem, dens_sem = refs[PLACES:]
    home_copy = pltpu.make_async_copy(home_hbm, home_ref, home_sem)
    home_copy.start()
    dens_copy = pltpu.make_async_copy(dens_hbm, dens_ref, dens_sem)
    dens_copy.start()
    position = lax.axis_index("gx")
    row = lax.broadcasted_iota(jnp.int32, (8, 128), 0)
    home_copy.wait()
    chosen = []
    odd = (position & 1) == 1
    for (step, odd_step), out_ref in zip(MOVES + ((0, 0),), outs):
        target = (position + jnp.where(odd, odd_step, step) + GROUP) & (GROUP - 1)
        bricks = find_bricks(home_ref, target)
        labels = [slot_label(home_ref, brick) for brick in bricks]
        out_ref[CAP * ROWS] = jnp.where(row == 0, labels[0], labels[1]).astype(jnp.float32)
        chosen.append([jnp.minimum(brick, BRICKS - 1) for brick in bricks])
    dens_copy.wait()
    for out_ref, bricks in zip(outs, chosen):
        for place, brick in enumerate(bricks):
            out_ref[pl.ds(place * ROWS, ROWS)] = dens_ref[brick]


def take_samples(jitter_ref, arrived, sample_ref, peak_ref):
    lane = lax.broadcasted_iota(jnp.int32, (8, 128), 1)
    plane = (lane >> 3) & 7
    collision = (lane & 7) * STRIDE
    jitter = jnp.concatenate([jitter_ref[...], jitter_ref[...]], axis=1)
    slots = []
    for source_ref in arrived:
        for place in range(CAP):
            label = source_ref[CAP * ROWS, place : place + 1, 0:1][0, 0]
            slots.append(label.astype(jnp.int32))
    for number, slot in enumerate(slots):
        source_ref, place = arrived[number // CAP], number % CAP
        for quarter in range(QUARTERS):
            moved = jnp.take_along_axis(
                jitter[quarter * 8 : (quarter + 1) * 8],
                slot * 8 + plane,
                axis=1,
                mode="promise_in_bounds",
            )
            where_at = collision + moved
            samples = None
            peak = None
            for x in range(8):
                cells = source_ref[place * ROWS + x * QUARTERS + quarter]
                taken = jnp.take_along_axis(cells, where_at, axis=1, mode="promise_in_bounds")
                samples = taken if x == 0 else jnp.where(plane == x, taken, samples)
                peak = cells if x == 0 else jnp.maximum(peak, cells)
            sample_ref[slot, quarter] = samples
            peak_ref[quarter, pl.ds(slot, 1), :] = jnp.max(peak, axis=0, keepdims=True)


def stay_kernel(jitter_ref, stayed, sample_ref, peak_ref):
    take_samples(jitter_ref, [stayed], sample_ref, peak_ref)


def early_kernel(jitter_ref, stay_samples, stay_peaks, *refs):
    del stay_samples, stay_peaks
    arrived, (sample_ref, peak_ref) = refs[: len(EARLY)], refs[len(EARLY) :]
    take_samples(jitter_ref, arrived, sample_ref, peak_ref)


def late_kernel(jitter_ref, early_samples, early_peaks, *refs):
    count = len(LATE)
    arrived = refs[:count]
    outs = refs[count : count + LAYERS]
    sample_ref, peak_ref = refs[count + LAYERS :]
    sample_ref[...] = early_samples[...]
    peak_ref[...] = early_peaks[...]
    take_samples(jitter_ref, arrived, sample_ref, peak_ref)
    layer = lax.axis_index("gz")
    lane = lax.broadcasted_iota(jnp.int32, (8, 128), 1)
    quarters = [layer] + [look_up(table, layer) for table in SENDS]
    for quarter, out_ref in zip(quarters, outs):
        for tile in range(TILES):
            out_ref[tile] = jnp.where(
                lane < 64, sample_ref[2 * tile, quarter], sample_ref[2 * tile + 1, quarter]
            )
        peak = jnp.max(peak_ref[quarter, :BRICKS], axis=1, keepdims=True)
        out_ref[TILES] = jnp.broadcast_to(peak, (8, 128))


def render_kernel(*refs):
    out_ref, held_ref = refs[LAYERS:]
    layer = lax.axis_index("gz")
    sources = [layer]
    for table in SENDS:
        sources.append(look_up([table.index(place) for place in range(LAYERS)], layer))
    for source, message in zip(sources, refs[:LAYERS]):
        held_ref[source] = message[...]
    lane = lax.broadcasted_iota(jnp.int32, (8, 128), 1)
    tiles = TILES
    peak = held_ref[0, tiles]
    for depth in range(1, LAYERS):
        peak = jnp.maximum(peak, held_ref[depth, tiles])
    absorb = jnp.float32(DEPTH_GAIN / (8 * LAYERS))
    light = jnp.zeros((8, 128), jnp.float32)
    cover = jnp.zeros((8, 128), jnp.float32)
    picked = [(lane & 3) * 32 + x * 8 for x in range(PIXEL)]
    for tile in range(tiles):
        majorant = jnp.where(lane < 64, peak[2 * tile : 2 * tile + 1], peak[2 * tile + 1 : 2 * tile + 2])
        scale = absorb / majorant
        through = None
        radiance = None
        for depth in range(LAYERS):
            samples = held_ref[depth, tile]
            after = pltpu.roll(samples, 127, 1)
            ratio = samples * scale
            next_ratio = after * scale
            passed = 1.0 - ratio
            shone = ratio * (GLOW * samples) + passed * (next_ratio * (GLOW * after))
            passed = passed * (1.0 - next_ratio)
            for span in (2, 4):
                shone = shone + passed * pltpu.roll(shone, 128 - span, 1)
                passed = passed * pltpu.roll(passed, 128 - span, 1)
            if depth == 0:
                through, radiance = passed, shone
            else:
                radiance = radiance + through * shone
                through = through * passed
        pooled = []
        for field in (radiance, 1.0 - through):
            parts = [
                jnp.take_along_axis(field, where_at, axis=1, mode="promise_in_bounds")
                for where_at in picked
            ]
            pooled.append((parts[0] + parts[1]) + (parts[2] + parts[3]))
        here = (lane >> 2) == tile
        light = jnp.where(here, pooled[0], light)
        cover = jnp.where(here, pooled[1], cover)
    mean = jnp.float32(1.0 / (PIXEL * PIXEL))
    for number, field in enumerate((light, cover)):
        for pixel in range(8 // PIXEL):
            rows = field[pixel * PIXEL : (pixel + 1) * PIXEL, :16]
            out_ref[number, pixel : pixel + 1, :] = jnp.sum(rows, axis=0, keepdims=True) * mean


def shards(sim_density, brick_home, jitter):
    home = pltpu.with_memory_space_constraint(brick_home.reshape(BRICKS), pltpu.HBM)
    density = pltpu.with_memory_space_constraint(
        sim_density.reshape(BRICKS, ROWS, 8, 128), pltpu.HBM
    )
    vmem = pl.BlockSpec(memory_space=pltpu.VMEM)
    hbm = pl.BlockSpec(memory_space=pltpu.HBM)
    params = pltpu.CompilerParams(vmem_limit_bytes=VMEM_BYTES)
    box = jax.ShapeDtypeStruct((CAP * ROWS + 1, 8, 128), jnp.float32)
    packed = pl.pallas_call(
        pack_kernel,
        out_shape=[box] * PLACES,
        in_specs=[hbm, hbm],
        out_specs=[vmem] * PLACES,
        scratch_shapes=[
            pltpu.SMEM((BRICKS,), jnp.int32),
            pltpu.VMEM((BRICKS, ROWS, 8, 128), jnp.float32),
            pltpu.SemaphoreType.DMA,
            pltpu.SemaphoreType.DMA,
        ],
        compiler_params=params,
        name="pack",
    )(home, density)
    arrived = []
    for move, bricks in zip(MOVES, packed):
        pairs = [(source, (source + move[source % 2]) % GROUP) for source in range(GROUP)]
        arrived.append(lax.ppermute(bricks, "gx", pairs))
    sample_box = (BRICKS + 1, QUARTERS, 8, 128)
    peak_box = (QUARTERS, 2 * BRICKS, 128)
    boxes = [
        jax.ShapeDtypeStruct(sample_box, jnp.float32),
        jax.ShapeDtypeStruct(peak_box, jnp.float32),
    ]
    stayed = pl.pallas_call(
        stay_kernel,
        out_shape=boxes,
        in_specs=[vmem] * 2,
        out_specs=[vmem] * 2,
        compiler_params=params,
        name="stay",
    )(jitter.T, packed[-1])
    gathered = pl.pallas_call(
        early_kernel,
        out_shape=boxes,
        in_specs=[vmem] * (3 + len(EARLY)),
        out_specs=[vmem] * 2,
        input_output_aliases={1: 0, 2: 1},
        compiler_params=params,
        name="early",
    )(jitter.T, *stayed, *[arrived[number] for number in EARLY])
    messages = pl.pallas_call(
        late_kernel,
        out_shape=[jax.ShapeDtypeStruct((TILES + 1, 8, 128), jnp.float32)] * LAYERS,
        in_specs=[vmem] * (3 + len(LATE)),
        out_specs=[vmem] * LAYERS,
        scratch_shapes=[
            pltpu.VMEM(sample_box, jnp.float32),
            pltpu.VMEM(peak_box, jnp.float32),
        ],
        compiler_params=params,
        name="late",
    )(jitter.T, *gathered, *[arrived[number] for number in LATE])
    others = []
    for table, message in zip(SENDS, messages[1:]):
        others.append(lax.ppermute(message, "gz", list(enumerate(table))))
    image = pl.pallas_call(
        render_kernel,
        out_shape=jax.ShapeDtypeStruct((2, 8 // PIXEL, 16), jnp.float32),
        in_specs=[vmem] * LAYERS,
        out_specs=vmem,
        scratch_shapes=[pltpu.VMEM((LAYERS, TILES + 1, 8, 128), jnp.float32)],
        compiler_params=params,
        name="render",
    )(messages[0], *others)
    return jnp.transpose(image, (0, 2, 1))


def solution(mesh):
    in_specs = (P("gx", None, "gy", "gz"), P("gx", "gy", "gz"), P("gx", "gy"))
    out_specs = P(None, "gx", ("gy", "gz"))
    return jax.shard_map(shards, mesh=mesh, in_specs=in_specs, out_specs=out_specs, check_vma=False)
```

```python
import jax
import jax.numpy as jnp
from jax import lax
from jax.experimental import pallas as pl
from jax.experimental.pallas import tpu as pltpu
from jax.sharding import PartitionSpec as P

STRIDE = 16
MT = 8
PIXEL = 4
GLOW = 5.0
DEPTH_GAIN = 12.0

BRICKS = 8
ROWS = 32
QUARTERS = 4
CAP = 2
GROUP = 16
LAYERS = 4
NONE = BRICKS
VMEM_BYTES = 4 << 20

MOVES = ((1, 1), (-2, -2), (2, 2), (-1, -1))
EARLY = (0, 1)
LATE = (2, 3)
PLACES = len(MOVES) + 1
SENDS = ((3, 2, 0, 1), (2, 3, 1, 0), (1, 0, 3, 2))
TILES = BRICKS // 2


def look_up(table, position):
    packed = sum(entry << (4 * index) for index, entry in enumerate(table))
    return (jnp.int32(packed) >> (4 * position)) & 15


def find_bricks(home_ref, target):
    first = jnp.int32(NONE)
    second = jnp.int32(NONE)
    for brick in range(BRICKS - 1, -1, -1):
        hit = (home_ref[brick] >> 3) == target
        second = jnp.where(hit, first, second)
        first = jnp.where(hit, jnp.int32(brick), first)
    return first, second


def slot_label(home_ref, brick):
    held = home_ref[jnp.minimum(brick, BRICKS - 1)] & (BRICKS - 1)
    return jnp.where(brick < BRICKS, held, NONE)


def pack_kernel(home_hbm, dens_hbm, *refs):
    outs = refs[:PLACES]
    home_ref, dens_ref, home_sem, dens_sem = refs[PLACES:]
    home_copy = pltpu.make_async_copy(home_hbm, home_ref, home_sem)
    home_copy.start()
    dens_copy = pltpu.make_async_copy(dens_hbm, dens_ref, dens_sem)
    dens_copy.start()
    position = lax.axis_index("gx")
    row = lax.broadcasted_iota(jnp.int32, (8, 128), 0)
    home_copy.wait()
    chosen = []
    odd = (position & 1) == 1
    for (step, odd_step), out_ref in zip(MOVES + ((0, 0),), outs):
        target = (position + jnp.where(odd, odd_step, step) + GROUP) & (GROUP - 1)
        bricks = find_bricks(home_ref, target)
        labels = [slot_label(home_ref, brick) for brick in bricks]
        out_ref[CAP * ROWS] = jnp.where(row == 0, labels[0], labels[1]).astype(jnp.float32)
        chosen.append([jnp.minimum(brick, BRICKS - 1) for brick in bricks])
    dens_copy.wait()
    for out_ref, bricks in zip(outs, chosen):
        for place, brick in enumerate(bricks):
            out_ref[pl.ds(place * ROWS, ROWS)] = dens_ref[brick]


def take_samples(jitter_ref, arrived, sample_ref, peak_ref):
    lane = lax.broadcasted_iota(jnp.int32, (8, 128), 1)
    plane = (lane >> 3) & 7
    collision = (lane & 7) * STRIDE
    jitter = jnp.concatenate([jitter_ref[...], jitter_ref[...]], axis=1)
    slots = []
    for source_ref in arrived:
        for place in range(CAP):
            label = source_ref[CAP * ROWS, place : place + 1, 0:1][0, 0]
            slots.append(label.astype(jnp.int32))
    for number, slot in enumerate(slots):
        source_ref, place = arrived[number // CAP], number % CAP
        for quarter in range(QUARTERS):
            moved = jnp.take_along_axis(
                jitter[quarter * 8 : (quarter + 1) * 8],
                slot * 8 + plane,
                axis=1,
                mode="promise_in_bounds",
            )
            where_at = collision + moved
            samples = None
            peak = None
            for x in range(8):
                cells = source_ref[place * ROWS + x * QUARTERS + quarter]
                taken = jnp.take_along_axis(cells, where_at, axis=1, mode="promise_in_bounds")
                samples = taken if x == 0 else jnp.where(plane == x, taken, samples)
                peak = cells if x == 0 else jnp.maximum(peak, cells)
            sample_ref[slot, quarter] = samples
            peak_ref[quarter, pl.ds(slot, 1), :] = jnp.max(peak, axis=0, keepdims=True)


def stay_kernel(jitter_ref, stayed, sample_ref, peak_ref):
    take_samples(jitter_ref, [stayed], sample_ref, peak_ref)


def early_kernel(jitter_ref, stay_samples, stay_peaks, *refs):
    del stay_samples, stay_peaks
    arrived, (sample_ref, peak_ref) = refs[: len(EARLY)], refs[len(EARLY) :]
    take_samples(jitter_ref, arrived, sample_ref, peak_ref)


def late_kernel(jitter_ref, early_samples, early_peaks, *refs):
    count = len(LATE)
    arrived = refs[:count]
    outs = refs[count : count + LAYERS]
    sample_ref, peak_ref = refs[count + LAYERS :]
    sample_ref[...] = early_samples[...]
    peak_ref[...] = early_peaks[...]
    take_samples(jitter_ref, arrived, sample_ref, peak_ref)
    layer = lax.axis_index("gz")
    lane = lax.broadcasted_iota(jnp.int32, (8, 128), 1)
    quarters = [layer] + [look_up(table, layer) for table in SENDS]
    for quarter, out_ref in zip(quarters, outs):
        for tile in range(TILES):
            out_ref[tile] = jnp.where(
                lane < 64, sample_ref[2 * tile, quarter], sample_ref[2 * tile + 1, quarter]
            )
        peak = jnp.max(peak_ref[quarter, :BRICKS], axis=1, keepdims=True)
        out_ref[TILES] = jnp.broadcast_to(peak, (8, 128))


def render_kernel(*refs):
    out_ref, held_ref = refs[LAYERS:]
    layer = lax.axis_index("gz")
    sources = [layer]
    for table in SENDS:
        sources.append(look_up([table.index(place) for place in range(LAYERS)], layer))
    for source, message in zip(sources, refs[:LAYERS]):
        held_ref[source] = message[...]
    lane = lax.broadcasted_iota(jnp.int32, (8, 128), 1)
    tiles = TILES
    peak = held_ref[0, tiles]
    for depth in range(1, LAYERS):
        peak = jnp.maximum(peak, held_ref[depth, tiles])
    absorb = jnp.float32(DEPTH_GAIN / (8 * LAYERS))
    light = jnp.zeros((8, 128), jnp.float32)
    cover = jnp.zeros((8, 128), jnp.float32)
    picked = [(lane & 3) * 32 + x * 8 for x in range(PIXEL)]
    for tile in range(tiles):
        majorant = jnp.where(lane < 64, peak[2 * tile : 2 * tile + 1], peak[2 * tile + 1 : 2 * tile + 2])
        scale = absorb / majorant
        through = None
        radiance = None
        for depth in range(LAYERS):
            samples = held_ref[depth, tile]
            after = pltpu.roll(samples, 127, 1)
            ratio = samples * scale
            next_ratio = after * scale
            passed = 1.0 - ratio
            shone = ratio * (GLOW * samples) + passed * (next_ratio * (GLOW * after))
            passed = passed * (1.0 - next_ratio)
            for span in (2, 4):
                shone = shone + passed * pltpu.roll(shone, 128 - span, 1)
                passed = passed * pltpu.roll(passed, 128 - span, 1)
            if depth == 0:
                through, radiance = passed, shone
            else:
                radiance = radiance + through * shone
                through = through * passed
        pooled = []
        for field in (radiance, 1.0 - through):
            parts = [
                jnp.take_along_axis(field, where_at, axis=1, mode="promise_in_bounds")
                for where_at in picked
            ]
            pooled.append((parts[0] + parts[1]) + (parts[2] + parts[3]))
        here = (lane >> 2) == tile
        light = jnp.where(here, pooled[0], light)
        cover = jnp.where(here, pooled[1], cover)
    mean = jnp.float32(1.0 / (PIXEL * PIXEL))
    for number, field in enumerate((light, cover)):
        for pixel in range(8 // PIXEL):
            rows = field[pixel * PIXEL : (pixel + 1) * PIXEL, :16]
            out_ref[number, pixel : pixel + 1, :] = jnp.sum(rows, axis=0, keepdims=True) * mean


def shards(sim_density, brick_home, jitter):
    home = pltpu.with_memory_space_constraint(brick_home.reshape(BRICKS), pltpu.HBM)
    density = pltpu.with_memory_space_constraint(
        sim_density.reshape(BRICKS, ROWS, 8, 128), pltpu.HBM
    )
    vmem = pl.BlockSpec(memory_space=pltpu.VMEM)
    hbm = pl.BlockSpec(memory_space=pltpu.HBM)
    params = pltpu.CompilerParams(vmem_limit_bytes=VMEM_BYTES)
    box = jax.ShapeDtypeStruct((CAP * ROWS + 1, 8, 128), jnp.float32)
    packed = pl.pallas_call(
        pack_kernel,
        out_shape=[box] * PLACES,
        in_specs=[hbm, hbm],
        out_specs=[vmem] * PLACES,
        scratch_shapes=[
            pltpu.SMEM((BRICKS,), jnp.int32),
            pltpu.VMEM((BRICKS, ROWS, 8, 128), jnp.float32),
            pltpu.SemaphoreType.DMA,
            pltpu.SemaphoreType.DMA,
        ],
        compiler_params=params,
        name="pack",
    )(home, density)
    arrived = []
    for move, bricks in zip(MOVES, packed):
        pairs = [(source, (source + move[source % 2]) % GROUP) for source in range(GROUP)]
        arrived.append(lax.ppermute(bricks, "gx", pairs))
    sample_box = (BRICKS + 1, QUARTERS, 8, 128)
    peak_box = (QUARTERS, 2 * BRICKS, 128)
    boxes = [
        jax.ShapeDtypeStruct(sample_box, jnp.float32),
        jax.ShapeDtypeStruct(peak_box, jnp.float32),
    ]
    stayed = pl.pallas_call(
        stay_kernel,
        out_shape=boxes,
        in_specs=[vmem] * 2,
        out_specs=[vmem] * 2,
        compiler_params=params,
        name="stay",
    )(jitter.T, packed[-1])
    gathered = pl.pallas_call(
        early_kernel,
        out_shape=boxes,
        in_specs=[vmem] * (3 + len(EARLY)),
        out_specs=[vmem] * 2,
        input_output_aliases={1: 0, 2: 1},
        compiler_params=params,
        name="early",
    )(jitter.T, *stayed, *[arrived[number] for number in EARLY])
    messages = pl.pallas_call(
        late_kernel,
        out_shape=[jax.ShapeDtypeStruct((TILES + 1, 8, 128), jnp.float32)] * LAYERS,
        in_specs=[vmem] * (3 + len(LATE)),
        out_specs=[vmem] * LAYERS,
        scratch_shapes=[
            pltpu.VMEM(sample_box, jnp.float32),
            pltpu.VMEM(peak_box, jnp.float32),
        ],
        compiler_params=params,
        name="late",
    )(jitter.T, *gathered, *[arrived[number] for number in LATE])
    others = []
    for table, message in zip(SENDS, messages[1:]):
        others.append(lax.ppermute(message, "gz", list(enumerate(table))))
    image = pl.pallas_call(
        render_kernel,
        out_shape=jax.ShapeDtypeStruct((2, 8 // PIXEL, 16), jnp.float32),
        in_specs=[vmem] * LAYERS,
        out_specs=vmem,
        scratch_shapes=[pltpu.VMEM((LAYERS, TILES + 1, 8, 128), jnp.float32)],
        compiler_params=params,
        name="render",
    )(messages[0], *others)
    return jnp.transpose(image, (0, 2, 1))


def solution(mesh):
    in_specs = (P("gx", None, "gy", "gz"), P("gx", "gy", "gz"), P("gx", "gy"))
    out_specs = P(None, "gx", ("gy", "gz"))
    return jax.shard_map(shards, mesh=mesh, in_specs=in_specs, out_specs=out_specs, check_vma=False)
```
